32 devices in a mesh: sta: 8 (over z, x), seg: 4 (over y, core).
Axes of the slice: x: 2, y: 2, z: 4, core: 2. Of those that a mesh axis runs over, the one named last changes fastest.
Arguments:
- records: bfloat16 [128, 32, 4096], P('sta', 'seg'), may hold values from -6 to 6
- fir_taps: bfloat16 [32], replicated, may hold values from -1 to 1
- counts: int32 [128], replicated, may hold values from 1 to 32
- pair_blocks: int32 [16, 2], replicated, may hold values from 0 to 7, as said below
- owners: int32 [16, 1], replicated, may hold values from 0 to 7; in each aligned block of 16 rows (0 to 15, 16 to 31, ...) at most 4 rows name the same one
Outputs:
- correlation: float32 [32, 512, 256], P('sta', None, 'seg')
The draws below stay inside these ranges and needn't reach their ends.
Inputs may be any that keep to these rules, and one draw needn't show every extreme that they name: `pair_blocks`: each row names two station blocks at most one step apart in row and in column of a grid 8 blocks wide (block = 8 * row + column); every block is the first of exactly two rows. `owners`: every owner is named by 1 to 4 rows, a bound that some block reaches. A station's record is valid in segments 0 to counts - 1.
All inputs are finite; a program needn't handle non-finite values.
Results may differ from the reference program's by a relative error of at most 0.0089.
Values may be sent and summed in bfloat16 or wider, within the bound.
A program may use at most 192 MiB of HBM per device.

```python
import math
import jax
import jax.numpy as jnp
import numpy as np
from jax import lax

BLK = 16
SEGLEN = 1024
DEC = 4
TAPS = 32
NLAG = 512
CAP = 4
STATIONS = 128
SEGMENTS = 32
RAWLEN = 4096
NF = 512
PAIRS = 16
N_STA = 8


def draw_pair_blocks(key, part):
    key_first, key_second, key_col, key_row = jax.random.split(key, 4)
    first_half = jax.random.permutation(key_first, N_STA).astype(jnp.int32)
    second_half = jax.random.permutation(key_second, N_STA).astype(jnp.int32)
    first_block = jnp.concatenate([first_half, second_half]).astype(jnp.int32)
    grid_rows = N_STA // 8
    column = first_block % 8
    row_id = first_block // 8
    col_step = jax.random.randint(key_col, (PAIRS,), -1, 2).astype(jnp.int32)
    row_step = jax.random.randint(key_row, (PAIRS,), -1, 2).astype(jnp.int32)
    other = jnp.clip(row_id + row_step, 0, grid_rows - 1) * 8 + jnp.clip(column + col_step, 0, 7)
    return jnp.stack([first_block, other.astype(jnp.int32)], axis=1).astype(jnp.int32)


def plant(array, stream_key, low, high):
    dims = array.shape
    place = [jax.random.randint(jax.random.fold_in(stream_key, axis), (), 0, dims[axis]) for axis in range(len(dims))]
    array = array.at[tuple(place)].set(low)
    longest = dims.index(max(dims))
    place[longest] = (place[longest] + 1) % dims[longest]
    return array.at[tuple(place)].set(high)


def block_scale(stream_key, dims, cuts, smallest, largest):
    gain = 1.0
    for axis_at, parts in cuts:
        draws = jax.random.uniform(jax.random.fold_in(jax.random.fold_in(stream_key, 6), axis_at), (parts,), jnp.float32, smallest / len(cuts), largest / len(cuts))
        gain = gain * jnp.repeat(jnp.exp(draws), dims[axis_at] // parts).reshape((-1,) + (1,) * (len(dims) - 1 - axis_at))
    return gain


def shared_out(own_key, own, number, rows, amount, top, most, lean):
    ranking = jax.random.permutation(own_key, amount)
    packed, usual = portions_of(amount, rows * top, most, lean, True), portions_of(amount, rows * top, most, lean, False)
    places = jnp.arange(amount)

    def named(tallies, turn):
        used = int((tallies > 0).sum())
        fixed = max(1, used // 4)
        passed = fixed + (places - fixed + turn * (used - fixed)) % max(1, amount - fixed)
        return jnp.zeros((amount,), jnp.int32).at[ranking[jnp.where(places < fixed, places, passed)]].set(jnp.asarray(tallies, jnp.int32))

    tallies = jnp.where(number % 4 == 0, named(packed, number // 4), named(usual, number - number // 4 - 1))
    mixed = jax.random.permutation(jax.random.fold_in(own, 3), amount)
    giver, sink = mixed[0:amount // 2 * 2:2], mixed[1:amount // 2 * 2:2]
    room = jnp.minimum(tallies[giver] - 1, most - tallies[sink]) // 2
    room = jnp.where((giver == ranking[0]) | (sink == ranking[0]) | (tallies[sink] == 0), 0, jnp.maximum(room, 0))
    passed = jax.random.randint(jax.random.fold_in(own, 4), (amount // 2,), 0, 1 << 20) % (room + 1)
    tallies = tallies.at[giver].add(-passed).at[sink].add(passed)
    members = jnp.searchsorted(jnp.cumsum(tallies), jnp.arange(rows * top), side="right").astype(jnp.int32)
    listing = members.reshape(top, rows).T
    listing = listing[jax.random.permutation(jax.random.fold_in(own, 1), rows)]
    turn = jax.random.randint(jax.random.fold_in(own, 2), (rows, 1), 0, top)
    return jnp.take_along_axis(listing, (jnp.arange(top)[None, :] + turn) % top, axis=1)


def portions_of(number_of, total, limit, slope, full):
    weights = [(1 << 20) // math.isqrt(standing ** slope) + 1 for standing in range(1, number_of + 1)]
    largest = limit if full else min(limit, max(-(-total // number_of), total * weights[0] // sum(weights)))
    least = 1 if total - largest >= number_of - 1 else 0
    holding, rest = [largest] + [least] * (number_of - 1), total - largest - least * (number_of - 1)
    while rest > 0:
        candidates = [i for i in range(1, number_of) if holding[i] < largest] or [i for i in range(1, number_of) if holding[i] < limit]
        pool, remaining = sum([weights[i] for i in candidates]), rest
        for i in candidates:
            extra = min(limit - holding[i], max(1, remaining * weights[i] // pool), rest)
            holding[i] = holding[i] + extra
            rest = rest - extra
    return np.array(holding)


def centred(key, dims, spread, bound, shards=(), held_as=jnp.bfloat16):
    array = spread * jax.random.normal(key, dims, jnp.float32)
    if shards:
        array = array * block_scale(key, dims, shards, -0.22, 0.18)
    return jnp.clip(array, -bound, bound).astype(held_as)


def setup_inputs(seed: int = 0) -> dict:
    arg_keys = jax.random.split(jax.random.key(seed), 6)
    records = centred(arg_keys[0], (STATIONS, SEGMENTS, RAWLEN), 1.0, 6.0, ((0, 8), (1, 4)))
    fir_taps = centred(arg_keys[1], (TAPS,), TAPS ** -0.5, 1.0)
    counts = plant(jax.random.randint(arg_keys[2], (STATIONS,), 1, SEGMENTS + 1), jax.random.fold_in(arg_keys[2], 1), 1, SEGMENTS).astype(jnp.int32)
    pair_blocks = draw_pair_blocks(jax.random.fold_in(arg_keys[5], 71), 0)
    owners_keys = jax.random.split(jax.random.fold_in(arg_keys[4], 1), PAIRS // PAIRS)
    owners_turns = jax.random.permutation(jax.random.fold_in(arg_keys[4], 3), PAIRS // PAIRS)
    owners = jax.vmap(lambda own, number: shared_out(jax.random.fold_in(arg_keys[4], 2), own, number, PAIRS, N_STA, 1, CAP, 2))(owners_keys, owners_turns).reshape((PAIRS, 1))
    return dict(records=records, fir_taps=fir_taps, counts=counts, pair_blocks=pair_blocks, owners=owners)


WATER = 0.1
TINY = 1e-06

def forward_table(seglen):
    sample_pos = jnp.arange(seglen, dtype=jnp.int32)
    freq_pos = jnp.arange(seglen // 2, dtype=jnp.int32)
    phase = sample_pos[:, None] * freq_pos[None, :] % seglen
    angle = phase.astype(jnp.float32) * (2.0 * math.pi / seglen)
    return jnp.concatenate([jnp.cos(angle), -jnp.sin(angle)], axis=1).astype(jnp.bfloat16)

def inverse_table(seglen, nlag):
    freq_pos = jnp.arange(seglen // 2, dtype=jnp.int32)
    lag_pos = jnp.arange(nlag, dtype=jnp.int32) - nlag // 2
    phase = jnp.mod(freq_pos[:, None] * lag_pos[None, :], seglen)
    angle = phase.astype(jnp.float32) * (2.0 * math.pi / seglen)
    scale = 1.0 / math.sqrt(seglen // 2)
    both = jnp.stack([jnp.cos(angle) * scale, -jnp.sin(angle) * scale], axis=1)
    return both.reshape(seglen, nlag).astype(jnp.bfloat16)

def whiten(spectrum, nfreq):
    real_part = spectrum[:, :nfreq]
    imag_part = spectrum[:, nfreq:]
    magnitude = jnp.sqrt(real_part * real_part + imag_part * imag_part)
    mean_level = lax.optimization_barrier(jnp.mean(magnitude, axis=1, keepdims=True))
    divisor = magnitude + WATER * mean_level + TINY
    return spectrum / jnp.concatenate([divisor, divisor], axis=1)

def slot_tables(pair_blocks, owners, sta_count):
    owner_ids = owners[:, 0]
    position = jnp.arange(owner_ids.shape[0], dtype=jnp.int32)
    same_owner = (owner_ids[:, None] == owner_ids[None, :]) & (position[None, :] < position[:, None])
    rank_of = lax.optimization_barrier(jnp.sum(same_owner.astype(jnp.int32), axis=1))
    slot_of = owner_ids * CAP + rank_of
    slot_hit = slot_of[None, :] == jnp.arange(sta_count * CAP, dtype=jnp.int32)[:, None]
    first_block = lax.optimization_barrier(jnp.sum(jnp.where(slot_hit, pair_blocks[None, :, 0], 0), axis=1)).astype(jnp.int32)
    second_block = lax.optimization_barrier(jnp.sum(jnp.where(slot_hit, pair_blocks[None, :, 1], 0), axis=1)).astype(jnp.int32)
    live_mask = jnp.any(slot_hit, axis=1).astype(jnp.float32)
    return (first_block, second_block, live_mask)

def reference(records, fir_taps, counts, pair_blocks, owners):
    dft_table = forward_table(SEGLEN)
    taps_wide = fir_taps.astype(jnp.float32)

    def front(inputs):
        block_records, block_counts = inputs
        frames = block_records.astype(jnp.float32).reshape(BLK, SEGMENTS, SEGLEN, DEC)
        total = jnp.zeros((BLK, SEGMENTS, SEGLEN), jnp.float32)
        for tap_index in range(TAPS):
            back = tap_index // DEC
            lane = DEC - 1 - tap_index % DEC
            column = frames[:, :, :, lane]
            shifted = jnp.pad(column, ((0, 0), (0, 0), (back, 0)))[:, :, :SEGLEN]
            total = total + taps_wide[tap_index] * shifted
        samples = total.astype(jnp.bfloat16).reshape(BLK * SEGMENTS, SEGLEN)
        spectrum = jnp.dot(samples, dft_table, preferred_element_type=jnp.float32)
        white = whiten(spectrum, NF).reshape(BLK, SEGMENTS, 2 * NF)
        valid = jnp.arange(SEGMENTS, dtype=jnp.int32)[None, :] < block_counts[:, None]
        return (white * valid[:, :, None].astype(jnp.float32)).astype(jnp.bfloat16)
    whitened = lax.map(front, (records.reshape(N_STA, BLK, SEGMENTS, RAWLEN), counts.reshape(N_STA, BLK)))
    first_block, second_block, live_mask = slot_tables(pair_blocks, owners, N_STA)
    counts_grid = counts.reshape(N_STA, BLK)
    inv_table = inverse_table(SEGLEN, NLAG)

    def one_slot(inputs):
        first_one, second_one, live_one = inputs
        left = whitened[first_one].astype(jnp.float32)
        right = whitened[second_one].astype(jnp.float32)
        left_real, left_imag = (left[:, :, :NF], left[:, :, NF:])
        right_real, right_imag = (right[:, :, :NF], right[:, :, NF:])
        real_sum = jnp.einsum('isf,jsf->fij', left_real, right_real) + jnp.einsum('isf,jsf->fij', left_imag, right_imag)
        imag_sum = jnp.einsum('isf,jsf->fij', left_imag, right_real) - jnp.einsum('isf,jsf->fij', left_real, right_imag)
        common = jnp.minimum(counts_grid[first_one][:, None], counts_grid[second_one][None, :]).astype(jnp.float32)
        weight = live_one / common
        stacked = jnp.stack([real_sum * weight, imag_sum * weight], axis=1).astype(jnp.bfloat16)
        stacked = stacked.reshape(2 * NF, BLK * BLK)
        return jnp.dot(inv_table.T, stacked, preferred_element_type=jnp.float32)
    return lax.map(one_slot, (first_block, second_block, live_mask))
```

```python
import functools
import math

import jax
import jax.numpy as jnp
import ml_dtypes
import numpy as np
from jax import lax
from jax.experimental import pallas as pl
from jax.experimental.pallas import tpu as pltpu
from jax.sharding import PartitionSpec as P

DEC = 4
TAPS = 32
NLAG = 512
CAP = 4
WATER = 0.1
TINY = 1e-06
AXES = ("sta", "seg")
VMEM = pl.BlockSpec(memory_space=pltpu.VMEM)
SMEM = pl.BlockSpec(memory_space=pltpu.SMEM)
LIMIT = 50 * 2**20


def forward_rows(seglen):
    phase = np.arange(seglen // 2)[:, None] * np.arange(seglen)[None, :] % seglen
    angle = phase * (2.0 * math.pi / seglen)
    both = np.concatenate([np.cos(angle), -np.sin(angle)], axis=0)
    return both.astype(np.float32).astype(ml_dtypes.bfloat16)


def inverse_rows(seglen, nlag, width):
    nfreq = seglen // 2
    lag = np.arange(nlag) - nlag // 2
    angle = (lag[:, None] * np.arange(nfreq)[None, :] % seglen) * (2.0 * math.pi / seglen)
    scale = 1.0 / math.sqrt(nfreq)
    both = np.stack([np.cos(angle) * scale, -np.sin(angle) * scale], axis=1)
    both = both.reshape(nlag, 2, nfreq // width, width).transpose(0, 2, 1, 3)
    return both.reshape(nlag, 2 * nfreq).astype(np.float32).astype(ml_dtypes.bfloat16)


def spread_tables(block, segs):
    eye = np.einsum("ai,sz->aszi", np.eye(block), np.eye(segs)).reshape(block * segs, segs, block)
    by_i = np.broadcast_to(eye[..., None], eye.shape + (block,))
    by_j = np.broadcast_to(eye[:, :, None, :], eye.shape[:2] + (block, block))
    shape = (block * segs, segs * block * block)
    return tuple(t.reshape(shape).astype(ml_dtypes.bfloat16) for t in (by_i, by_j))


def front_kernel(block, segs, taps_ref, counts_ref, rec_ref, dft_ref, out_ref, samp_ref):
    rows = block * segs
    nblocks = rec_ref.shape[1] // (128 * DEC)
    nfreq = dft_ref.shape[0] // 2
    span = 128 * DEC
    out_pos = lax.broadcasted_iota(jnp.int32, (128, 128 + span), 0)
    window_pos = lax.broadcasted_iota(jnp.int32, (128, 128 + span), 1)
    tap_of = DEC * out_pos + DEC - 1 + 128 - window_pos
    fir = jnp.zeros((128, 128 + span), jnp.float32)
    for k in range(TAPS):
        fir = jnp.where(tap_of == k, taps_ref[k], fir)
    fir = fir.astype(jnp.bfloat16)
    for b in range(nblocks):
        low = max(b * span - 128, 0)
        window = rec_ref[:, low : (b + 1) * span]
        kept = fir if b else fir[:, 128:]
        dec = lax.dot_general(
            kept, window, (((1,), (1,)), ((), ())), preferred_element_type=jnp.float32
        )
        samp_ref[b * 128 : (b + 1) * 128, :] = dec.astype(jnp.bfloat16)
    spectrum = jnp.dot(dft_ref[...], samp_ref[...], preferred_element_type=jnp.float32)
    real, imag = spectrum[:nfreq], spectrum[nfreq:]
    magnitude = jnp.sqrt(real * real + imag * imag)
    mean_level = jnp.sum(magnitude, axis=0, keepdims=True) * (1.0 / nfreq)
    divisor = magnitude + WATER * mean_level + TINY
    lane = lax.broadcasted_iota(jnp.int32, (1, rows), 1)
    first = lax.axis_index("sta") * block
    limit = jnp.zeros((1, rows), jnp.int32)
    for i in range(block):
        limit = jnp.where(lane // segs == i, counts_ref[first + i], limit)
    valid = (lax.axis_index("seg") * segs + lane % segs < limit).astype(jnp.float32)
    out_real = (real / divisor * valid).astype(jnp.bfloat16)
    out_imag = (imag / divisor * valid).astype(jnp.bfloat16)
    if len(out_ref.shape) == 2:
        out_ref[:nfreq, :] = out_real
        out_ref[nfreq:, :] = out_imag
    else:
        width = out_ref.shape[1] // 2
        for d in range(out_ref.shape[0]):
            out_ref[d, :width, :] = out_real[d * width : (d + 1) * width]
            out_ref[d, width:, :] = out_imag[d * width : (d + 1) * width]


def cross_kernel(
    groups, segs, owners_ref, pairs_ref, counts_ref, band_ref, by_i_ref, by_j_ref,
    out_ref, left_ref, right_ref, made_ref, slot_ref, used_ref,
):
    npairs = owners_ref.shape[0]
    nslots = slot_ref.shape[0]
    nsta = used_ref.shape[0]
    block = counts_ref.shape[0] // nsta
    lanes = block * block
    width = band_ref.shape[1] // 2

    @pl.loop(0, nslots)
    def _(q):
        slot_ref[q] = -1

    @pl.loop(0, nsta)
    def _(o):
        used_ref[o] = 0

    @pl.loop(0, npairs)
    def _(p):
        owner = owners_ref[p, 0]
        slot_ref[owner * CAP + used_ref[owner]] = p
        used_ref[owner] = used_ref[owner] + 1

    @pl.loop(0, nsta)
    def _(b):
        held = band_ref[pl.ds(b * groups, groups)].reshape(groups * 2 * width, -1)
        for s in range(segs):
            cols = slice(s * lanes, (s + 1) * lanes)
            for table, into in ((by_i_ref, left_ref), (by_j_ref, right_ref)):
                wide = jnp.dot(held, table[:, cols], preferred_element_type=jnp.float32)
                into[b, s] = wide

    lane = lax.broadcasted_iota(jnp.int32, (1, lanes), 1)
    low = lax.broadcasted_iota(jnp.int32, (2 * width, 128), 1) < 64

    @pl.loop(0, nslots // 2)
    def _(t):
        for e in range(2):
            pair = slot_ref[2 * t + e]

            @pl.when(pair < 0)
            def _():
                made_ref[e] = jnp.zeros(made_ref.shape[1:], jnp.float32)

            @pl.when(pair >= 0)
            def _():
                first, second = pairs_ref[pair, 0], pairs_ref[pair, 1]
                real = jnp.zeros((width, lanes), jnp.float32)
                imag = jnp.zeros((width, lanes), jnp.float32)
                for s in range(segs):
                    for g in range(groups):
                        at = g * 2 * width
                        lr = left_ref[first, s, at : at + width, :]
                        li = left_ref[first, s, at + width : at + 2 * width, :]
                        rr = right_ref[second, s, at : at + width, :]
                        ri = right_ref[second, s, at + width : at + 2 * width, :]
                        real = real + lr * rr + li * ri
                        imag = imag + li * rr - lr * ri
                left_count = jnp.zeros((1, lanes), jnp.int32)
                right_count = jnp.zeros((1, lanes), jnp.int32)
                for i in range(block):
                    left_count = jnp.where(lane // block == i, counts_ref[first * block + i], left_count)
                    right_count = jnp.where(lane % block == i, counts_ref[second * block + i], right_count)
                factor = 1.0 / jnp.minimum(left_count, right_count).astype(jnp.float32)
                made_ref[e, :width] = real * factor
                made_ref[e, width:] = imag * factor

        owner, half = t // (CAP // 2), t % (CAP // 2)
        parts = lanes // 64
        for j in range(parts):
            cols = slice(j // 2 * 128, j // 2 * 128 + 128)
            zero, one = made_ref[0, :, cols], made_ref[1, :, cols]
            if j % 2:
                zero = pltpu.roll(zero, 64, 1)
            else:
                one = pltpu.roll(one, 64, 1)
            out_ref[owner * parts + j, half] = jnp.where(low, zero, one).astype(jnp.bfloat16)


def cross_plain(bands, counts, pair_blocks, owners, nsta, groups, segs, width):
    owner_ids = owners[:, 0]
    position = jnp.arange(owner_ids.shape[0], dtype=jnp.int32)
    same = (owner_ids[:, None] == owner_ids[None, :]) & (position[None, :] < position[:, None])
    slot_of = owner_ids * CAP + jnp.sum(same.astype(jnp.int32), axis=1)
    block = counts.shape[0] // nsta
    hit = (slot_of[:, None] == jnp.arange(nsta * CAP, dtype=jnp.int32)[None, :]).astype(jnp.bfloat16)
    blocks = jnp.arange(nsta, dtype=jnp.int32)
    data = bands.reshape(nsta, groups, 2, width, block, segs)
    grid = counts.reshape(nsta, block).astype(jnp.float32)
    sides, limits = [], []
    for side in range(2):
        pick = (pair_blocks[:, side][:, None] == blocks[None, :]).astype(jnp.bfloat16)
        chosen = jnp.einsum("pn,ngufis->pgufis", pick, data, preferred_element_type=jnp.float32)
        sides.append(chosen.astype(jnp.bfloat16))
        limits.append(jnp.sum(jnp.where(pick[:, :, None] > 0, grid[None], 0.0), axis=1))
    left, right = sides
    common = jnp.minimum(limits[0][:, None, :, None], limits[1][:, None, None, :])
    dot = functools.partial(jnp.einsum, "pgfis,pgfjs->pfij", preferred_element_type=jnp.float32)
    real = dot(left[:, :, 0], right[:, :, 0]) + dot(left[:, :, 1], right[:, :, 1])
    imag = dot(left[:, :, 1], right[:, :, 0]) - dot(left[:, :, 0], right[:, :, 1])
    made = jnp.stack([real / common, imag / common], axis=1).astype(jnp.bfloat16)
    slots = jnp.einsum("pq,pufl->qufl", hit, made.reshape(made.shape[:3] + (block * block,)), preferred_element_type=jnp.float32)
    slots = slots.astype(jnp.bfloat16).reshape(nsta, CAP, 2, width, groups, block * block // groups)
    return slots.transpose(0, 4, 2, 3, 1, 5).reshape(nsta * groups, 2 * width, CAP * block * block // groups)


def last_kernel(inv_ref, stack_ref, out_ref):
    result = jnp.dot(inv_ref[...], stack_ref[...], preferred_element_type=jnp.float32)
    lanes = out_ref.shape[2]
    for c in range(out_ref.shape[0]):
        out_ref[c] = result[:, c * lanes : (c + 1) * lanes]


def last_kernel_halves(inv_ref, stack_ref, out_ref):
    for h in range(stack_ref.shape[1]):
        held = stack_ref[:, h].reshape(-1, 128)
        result = jnp.dot(inv_ref[...], held, preferred_element_type=jnp.float32)
        out_ref[2 * h] = result[:, :64]
        out_ref[2 * h + 1] = result[:, 64:]


def local(records, fir_taps, counts, pair_blocks, owners):
    block, segs, raw = records.shape
    nsta, groups = lax.axis_size("sta"), lax.axis_size("seg")
    devices = nsta * groups
    seglen = raw // DEC
    nfreq = seglen // 2
    width = nfreq // devices
    rows = block * segs
    lanes = block * block
    params = pltpu.CompilerParams(vmem_limit_bytes=LIMIT)
    fast = width % 16 == 0 and lanes // groups == 64 and rows == 128
    bf16 = jnp.bfloat16

    shape = (devices, 2 * width, rows) if fast else (2 * nfreq, rows)
    white = pl.pallas_call(
        functools.partial(front_kernel, block, segs),
        out_shape=jax.ShapeDtypeStruct(shape, bf16),
        in_specs=[SMEM, SMEM, VMEM, VMEM],
        out_specs=VMEM,
        scratch_shapes=[pltpu.VMEM((seglen, rows), bf16)],
        compiler_params=params,
        name="front",
    )(fir_taps.astype(jnp.float32), counts, records.reshape(rows, raw), jnp.asarray(forward_rows(seglen)))
    if not fast:
        white = white.reshape(2, devices, width, rows).transpose(1, 0, 2, 3)
        white = white.reshape(devices, 2 * width, rows)
    bands = lax.all_to_all(white, AXES, 0, 0, tiled=True)
    if fast:
        by_i, by_j = (jnp.asarray(t) for t in spread_tables(block, segs))
        spread = pltpu.VMEM((nsta, segs, groups * 2 * width, lanes), jnp.float32)
        stacked = pl.pallas_call(
            functools.partial(cross_kernel, groups, segs),
            out_shape=jax.ShapeDtypeStruct((devices, CAP // 2, 2 * width, 128), bf16),
            in_specs=[SMEM, SMEM, SMEM, VMEM, VMEM, VMEM],
            out_specs=VMEM,
            scratch_shapes=[
                spread,
                spread,
                pltpu.VMEM((2, 2 * width, lanes), jnp.float32),
                pltpu.SMEM((nsta * CAP,), jnp.int32),
                pltpu.SMEM((nsta,), jnp.int32),
            ],
            compiler_params=params,
            name="cross",
        )(owners, pair_blocks, counts, bands, by_i, by_j)
    else:
        stacked = cross_plain(bands, counts, pair_blocks, owners, nsta, groups, segs, width)
    moved = lax.all_to_all(stacked, AXES, 0, 0, tiled=True)
    if not fast:
        moved = moved.reshape(2 * nfreq, CAP * lanes // groups)
    return pl.pallas_call(
        last_kernel_halves if fast else last_kernel,
        out_shape=jax.ShapeDtypeStruct((CAP, NLAG, lanes // groups), jnp.float32),
        in_specs=[VMEM, VMEM],
        out_specs=VMEM,
        compiler_params=params,
        name="last",
    )(jnp.asarray(inverse_rows(seglen, NLAG, width)), moved)


def solution(mesh):
    in_specs = (P("sta", "seg", None), P(), P(), P(), P())
    out_specs = P("sta", None, "seg")
    return jax.shard_map(local, mesh=mesh, in_specs=in_specs, out_specs=out_specs, check_vma=False)
```
